32 devices in a mesh: groups: 2 (over x), gx: 8 (over z, y), gy: 2 (over core).
Axes of the slice: x: 2, y: 2, z: 4, core: 2. Of those that a mesh axis runs over, the one named last changes fastest.
Arguments:
- tokens: bfloat16 [16, 14336], P(('groups', 'gy'), 'gx'), parts along dimension 0, may hold values from -6 to 6
- gate_weight: bfloat16 [14336, 26624], P('gx', 'gy'), may hold values from -0.046875 to 0.046875
- up_weight: bfloat16 [14336, 26624], P('gx', 'gy'), may hold values from -0.046875 to 0.046875
Outputs:
- hidden: bfloat16 [16, 26624], P(('groups', 'gx'), 'gy'), parts along dimension 0
The draws below stay inside these ranges and needn't reach their ends.
There are 2 independent parts, one for each index of `groups`. The reference program is written for one: setup_inputs(seed, part) draws one part's arguments, and reference() takes and returns one part's arrays. A program takes and returns all parts, laid end to end along the dimension named above; an argument that names none is the same for every part. Nothing has to cross between parts.
All inputs are finite; a program needn't handle non-finite values.
Results may differ from the reference program's by a relative error of at most 0.001.
Values may be sent and summed in bfloat16 or wider, within the bound.
No kernel may reach another device: no remote copies, remote signals or barrier semaphores. Data moves between devices by JAX's collectives and lax.ppermute only.
A program may use at most 192 MiB of HBM per device.

```python
import jax
import jax.numpy as jnp

D = 14336
FF = 26624
ROWS = 8


def strengthened(array, stream_key, source, target, blocks, factor):
    owner, partner = [(jnp.arange(array.shape[position]) // (array.shape[position] // blocks)).reshape([-1 if axis == position else 1 for axis in range(array.ndim)]) for position in (source, target)]
    chosen = jax.random.permutation(stream_key, blocks)[partner]
    strong = (owner == chosen) | (owner == (partner + blocks // 2) % blocks)
    return jnp.where(strong, factor * array, array)


def block_levels(key, dims, pieces, smallest, largest):
    level, own = 1.0, jax.random.fold_in(key, 6)
    for dim, shards_of in pieces:
        steps = jnp.exp(jax.random.uniform(jax.random.fold_in(own, dim), (shards_of,), jnp.float32, smallest / len(pieces), largest / len(pieces)))
        level = level * jnp.repeat(steps, dims[dim] // shards_of).reshape([-1 if axis == dim else 1 for axis in range(len(dims))])
    return level


def bell_draw(rng, shape, scale, limit, pieces=(), held_as=jnp.bfloat16):
    array = jax.random.normal(rng, shape, jnp.float32) * scale
    if len(pieces) > 0:
        array = block_levels(rng, shape, pieces, -0.22, 0.18) * array
    return jnp.clip(array, min=-limit, max=limit).astype(held_as)


def bell_draw_with(own_key, dims, width, limit, shards, heavy, held_as=jnp.bfloat16):
    result = width * jax.random.normal(own_key, dims, jnp.float32)
    if shards:
        result = result * block_levels(own_key, dims, shards, -0.22, 0.18)
    return jnp.clip(strengthened(result, jax.random.fold_in(own_key, 3), *heavy), -limit, limit).astype(held_as)


def setup_inputs(seed: int = 0, part: int = 0) -> dict:
    key_list = jax.random.split(jax.random.key(seed), 4)
    part_splits = jax.random.split(jax.random.fold_in(key_list[3], part), 4)
    return {
        "tokens": bell_draw_with(part_splits[0], (ROWS, D), 1.0, 6.0, ((0, 2), (1, 8)), (1, 0, 8, 2.0)),
        "gate_weight": bell_draw(key_list[1], (D, FF), D ** -0.5, 0.046875, ((0, 8), (1, 2))),
        "up_weight": bell_draw(key_list[2], (D, FF), D ** -0.5, 0.046875, ((0, 8), (1, 2))),
    }


def reference(tokens, gate_weight, up_weight):
    gate = jnp.dot(tokens, gate_weight, preferred_element_type=jnp.float32)
    up = jnp.dot(tokens, up_weight, preferred_element_type=jnp.float32)
    return (jax.nn.silu(gate) * up).astype(jnp.bfloat16)
```

```python
import functools

import jax
import jax.numpy as jnp
from jax import lax
from jax.experimental import pallas as pl
from jax.experimental.pallas import tpu as pltpu
from jax.sharding import PartitionSpec as P

LANES = 128


def masks(count, core):
    bits = [1 << b for b in range(count.bit_length() - 1)]
    if core % 2 and len(bits) > 1:
        bits[0], bits[1] = bits[1], bits[0]
    return bits


def column_block(width):
    units = width // LANES
    return LANES * max(d for d in range(1, min(units, 4) + 1) if units % d == 0)


def project_kernel(sizes, base_blocks, block, blocks, tokens_ref, gate_hbm, up_hbm, send_ref, keep_ref, rows_ref, buffer, sems):
    groups, gx, gy = sizes
    group, x, core = lax.axis_index("groups"), lax.axis_index("gx"), lax.axis_index("gy")
    base = group * base_blocks
    slots = buffer.shape[0]

    def copies(i, slot):
        columns = pl.ds(pl.multiple_of((base + i) * block, LANES), block)
        return [
            pltpu.make_async_copy(hbm.at[:, columns], buffer.at[slot, w], sems.at[slot, w])
            for w, hbm in enumerate((gate_hbm, up_hbm))
        ]

    for i in range(min(slots - 1, blocks)):
        for copy in copies(i, i):
            copy.start()

    rows = tokens_ref.shape[0]
    each = rows // (groups * gx)
    m = lax.broadcasted_iota(jnp.int32, (rows, rows), 0)
    source = lax.broadcasted_iota(jnp.int32, (rows, rows), 1)
    j, q, i = m // (groups * each), (m // each) % groups, m % each
    mine, other = masks(gx, 0), masks(gx, 1)
    flip = jnp.zeros_like(j)
    for n in range(len(mine)):
        bit = (j // (1 << (len(mine) - 1 - n))) % 2
        flip = flip + bit * jnp.where(core == 0, mine[n], other[n])
    wanted = ((group + q) % groups) * (gx * each) + (x ^ flip) * each + i
    pick = (source == wanted).astype(jnp.bfloat16)
    rows_ref[...] = jnp.dot(pick, tokens_ref[...], preferred_element_type=jnp.float32).astype(jnp.bfloat16)

    half = rows // 2

    def step(n, carry):
        slot = lax.rem(n, slots)

        @pl.when(n + slots - 1 < blocks)
        def _():
            for copy in copies(n + slots - 1, lax.rem(n + slots - 1, slots)):
                copy.start()

        columns = pl.ds(pl.multiple_of(n * block, LANES), block)
        for w, copy in enumerate(copies(n, slot)):
            copy.wait()
            total = jnp.dot(rows_ref[...], buffer[slot, w], preferred_element_type=jnp.float32)
            keep_ref[w, :, columns] = total[:half]
            send_ref[w, :, columns] = total[half:]
        return carry

    lax.fori_loop(0, blocks, step, 0)


def project(sizes, tokens, gate_weight, up_weight):
    rows, depth = tokens.shape
    width = gate_weight.shape[1] // sizes[0]
    block = column_block(width)
    blocks = width // block
    slots = min(4, blocks)
    shape = jax.ShapeDtypeStruct((2, rows // 2, width), jnp.float32)
    return pl.pallas_call(
        functools.partial(project_kernel, sizes, blocks, block, blocks),
        in_specs=[
            pl.BlockSpec(memory_space=pltpu.VMEM),
            pl.BlockSpec(memory_space=pl.ANY),
            pl.BlockSpec(memory_space=pl.ANY),
        ],
        out_specs=[pl.BlockSpec(memory_space=pltpu.VMEM)] * 2,
        out_shape=[shape, shape],
        scratch_shapes=[
            pltpu.VMEM((rows, depth), jnp.bfloat16),
            pltpu.VMEM((slots, 2, depth, block), jnp.bfloat16),
            pltpu.SemaphoreType.DMA((slots, 2)),
        ],
        cost_estimate=pl.CostEstimate(
            flops=4 * rows * depth * width, bytes_accessed=4 * depth * width, transcendentals=0
        ),
        compiler_params=pltpu.CompilerParams(vmem_limit_bytes=44 << 20),
    )(tokens, gate_weight, up_weight)


def per_device(sizes, tokens, gate_weight, up_weight):
    groups, gx, gy = sizes
    rows = lax.all_gather(tokens, ("groups", "gy"), axis=0, tiled=True)
    send, keep = project(sizes, rows, gate_weight, up_weight)
    phases = gx.bit_length() - 1
    for n in range(phases):
        pairs = [
            (x * gy + core, (x ^ masks(gx, core)[n]) * gy + core) for x in range(gx) for core in range(gy)
        ]
        total = keep + lax.ppermute(send, ("gx", "gy"), pairs)
        half = total.shape[1] // 2
        if n < phases - 1:
            keep, send = total[:, :half], total[:, half:]
    hidden = (jax.nn.silu(total[0]) * total[1]).astype(jnp.bfloat16)
    each = hidden.shape[0] // groups
    own, theirs = hidden[:each], hidden[each:]
    theirs = lax.ppermute(theirs, "groups", [(g, (g + 1) % groups) for g in range(groups)])
    first = lax.axis_index("groups") == 0
    return jnp.concatenate([jnp.where(first, own, theirs), jnp.where(first, theirs, own)], axis=1)


def solution(mesh):
    sizes = tuple(mesh.shape[name] for name in ("groups", "gx", "gy"))
    in_specs = (P(("groups", "gy"), "gx"), P("gx", "gy"), P("gx", "gy"))
    out_specs = P(("groups", "gx"), "gy")
    return jax.shard_map(
        functools.partial(per_device, sizes), mesh=mesh, in_specs=in_specs, out_specs=out_specs, check_vma=False
    )
```

```python
import functools

import jax
import jax.numpy as jnp
from jax import lax
from jax.experimental import pallas as pl
from jax.experimental.pallas import tpu as pltpu
from jax.sharding import PartitionSpec as P

LANES = 128


def masks(count, core):
    bits = [1 << b for b in range(count.bit_length() - 1)]
    if core % 2 and len(bits) > 1:
        bits[0], bits[1] = bits[1], bits[0]
    return bits


def column_block(width):
    units = width // LANES
    return LANES * max(d for d in range(1, min(units, 4) + 1) if units % d == 0)


def pick_rows(sizes, tokens):
    groups, gx, gy = sizes
    group, x, core = lax.axis_index("groups"), lax.axis_index("gx"), lax.axis_index("gy")
    rows = tokens.shape[0]
    each = rows // (groups * gx)
    m = lax.broadcasted_iota(jnp.int32, (rows, rows), 0)
    source = lax.broadcasted_iota(jnp.int32, (rows, rows), 1)
    j, q, i = m // (groups * each), (m // each) % groups, m % each
    mine, other = masks(gx, 0), masks(gx, 1)
    flip = jnp.zeros_like(j)
    for n in range(len(mine)):
        bit = (j // (1 << (len(mine) - 1 - n))) % 2
        flip = flip + bit * jnp.where(core == 0, mine[n], other[n])
    wanted = ((group + q) % groups) * (gx * each) + (x ^ flip) * each + i
    pick = (source == wanted).astype(jnp.bfloat16)
    return jnp.dot(pick, tokens, preferred_element_type=jnp.float32).astype(jnp.bfloat16)


def project_kernel(sizes, all_blocks, part, block, first, tokens_ref, gate_hbm, up_hbm, send_ref, keep_ref, rows_ref, buffer, sems):
    base = lax.axis_index("groups") * all_blocks + part[0]
    blocks = part[1] - part[0]
    slots = buffer.shape[0]

    def copies(i, slot):
        columns = pl.ds(pl.multiple_of((base + i) * block, LANES), block)
        return [
            pltpu.make_async_copy(hbm.at[:, columns], buffer.at[slot, w], sems.at[slot, w])
            for w, hbm in enumerate((gate_hbm, up_hbm))
        ]

    for i in range(min(slots - 1, blocks)):
        for copy in copies(i, i):
            copy.start()

    rows_ref[...] = pick_rows(sizes, tokens_ref[...]) if first else tokens_ref[...]
    half = rows_ref.shape[0] // 2

    def step(n, carry):
        slot = lax.rem(n, slots)

        @pl.when(n + slots - 1 < blocks)
        def _():
            for copy in copies(n + slots - 1, lax.rem(n + slots - 1, slots)):
                copy.start()

        columns = pl.ds(pl.multiple_of(n * block, LANES), block)
        for w, copy in enumerate(copies(n, slot)):
            copy.wait()
            total = jnp.dot(rows_ref[...], buffer[slot, w], preferred_element_type=jnp.float32)
            keep_ref[w, :, columns] = total[:half]
            send_ref[w, :, columns] = total[half:]
        return carry

    lax.fori_loop(0, blocks, step, 0)


def project(sizes, part, block, first, tokens, gate_weight, up_weight):
    rows, depth = tokens.shape
    all_blocks = gate_weight.shape[1] // (sizes[0] * block)
    blocks = part[1] - part[0]
    width = blocks * block
    slots = min(4, blocks)
    shape = jax.ShapeDtypeStruct((2, rows // 2, width), jnp.float32)
    return pl.pallas_call(
        functools.partial(project_kernel, sizes, all_blocks, part, block, first),
        in_specs=[
            pl.BlockSpec(memory_space=pltpu.VMEM),
            pl.BlockSpec(memory_space=pl.ANY),
            pl.BlockSpec(memory_space=pl.ANY),
        ],
        out_specs=[pl.BlockSpec(memory_space=pltpu.VMEM)] * 3,
        out_shape=[shape, shape, jax.ShapeDtypeStruct((rows, depth), jnp.bfloat16)],
        scratch_shapes=[
            pltpu.VMEM((slots, 2, depth, block), jnp.bfloat16),
            pltpu.SemaphoreType.DMA((slots, 2)),
        ],
        cost_estimate=pl.CostEstimate(
            flops=4 * rows * depth * width, bytes_accessed=4 * depth * width, transcendentals=0
        ),
        compiler_params=pltpu.CompilerParams(vmem_limit_bytes=44 << 20),
    )(tokens, gate_weight, up_weight)


def exchange(sizes, n, send):
    groups, gx, gy = sizes
    pairs = [(x * gy + core, (x ^ masks(gx, core)[n]) * gy + core) for x in range(gx) for core in range(gy)]
    return lax.ppermute(send, ("gx", "gy"), pairs)


def halves(total):
    half = total.shape[1] // 2
    return total[:, half:], total[:, :half]


def per_device(sizes, tokens, gate_weight, up_weight):
    groups, gx, gy = sizes
    tokens = lax.all_gather(tokens, ("groups", "gy"), axis=0, tiled=True)
    width = gate_weight.shape[1] // groups
    block = column_block(width)
    blocks = width // block
    cut = blocks * 9 // 13
    phases = gx.bit_length() - 1
    sums = []
    for first, part in ((True, (0, cut)), (False, (cut, blocks))):
        send, keep, tokens = project(sizes, part, block, first, tokens, gate_weight, up_weight)
        send, keep = halves(keep + exchange(sizes, 0, send))
        sums.append((send, keep))
    sums = [keep + exchange(sizes, 1, send) for send, keep in sums]
    total = jnp.concatenate(sums, axis=2)
    for n in range(2, phases):
        send, keep = halves(total)
        total = keep + exchange(sizes, n, send)
    hidden = (jax.nn.silu(total[0]) * total[1]).astype(jnp.bfloat16)
    each = hidden.shape[0] // groups
    own, theirs = hidden[:each], hidden[each:]
    theirs = lax.ppermute(theirs, "groups", [(g, (g + 1) % groups) for g in range(groups)])
    first = lax.axis_index("groups") == 0
    return jnp.concatenate([jnp.where(first, own, theirs), jnp.where(first, theirs, own)], axis=1)


def solution(mesh):
    sizes = tuple(mesh.shape[name] for name in ("groups", "gx", "gy"))
    in_specs = (P(("groups", "gy"), "gx"), P("gx", "gy"), P("gx", "gy"))
    out_specs = P(("groups", "gx"), "gy")
    return jax.shard_map(
        functools.partial(per_device, sizes), mesh=mesh, in_specs=in_specs, out_specs=out_specs, check_vma=False
    )
```

```python
import functools

import jax
import jax.numpy as jnp
from jax import lax
from jax.experimental import pallas as pl
from jax.experimental.pallas import tpu as pltpu
from jax.sharding import PartitionSpec as P

LANES = 128


def masks(count, core):
    bits = [1 << b for b in range(count.bit_length() - 1)]
    if core % 2 and len(bits) > 1:
        bits[0], bits[1] = bits[1], bits[0]
    return bits


def column_block(width):
    units = width // LANES
    return LANES * max(d for d in range(1, min(units, 4) + 1) if units % d == 0)


def weight_copies(weights, target, sems, column, block):
    columns = pl.ds(pl.multiple_of(column * block, LANES), block)
    return [pltpu.make_async_copy(w.at[:, columns], target.at[i], sems.at[i]) for i, w in enumerate(weights)]


def fetch_kernel(all_blocks, block, gate_hbm, up_hbm, ahead_ref, sems):
    base = lax.axis_index("groups") * all_blocks
    copies = []
    for n in range(ahead_ref.shape[0]):
        copies += weight_copies((gate_hbm, up_hbm), ahead_ref.at[n], sems.at[n], base + n, block)
    for copy in copies:
        copy.start()
    for copy in copies:
        copy.wait()


def fetch(all_blocks, block, ahead, gate_weight, up_weight):
    depth = gate_weight.shape[0]
    return pl.pallas_call(
        functools.partial(fetch_kernel, all_blocks, block),
        in_specs=[pl.BlockSpec(memory_space=pl.ANY)] * 2,
        out_specs=pl.BlockSpec(memory_space=pltpu.VMEM),
        out_shape=jax.ShapeDtypeStruct((ahead, 2, depth, block), jnp.bfloat16),
        scratch_shapes=[pltpu.SemaphoreType.DMA((ahead, 2))],
        cost_estimate=pl.CostEstimate(flops=0, bytes_accessed=4 * depth * ahead * block, transcendentals=0),
        compiler_params=pltpu.CompilerParams(vmem_limit_bytes=16 << 20),
    )(gate_weight, up_weight)


def pick_rows(sizes, tokens):
    groups, gx, gy = sizes
    group, x, core = lax.axis_index("groups"), lax.axis_index("gx"), lax.axis_index("gy")
    rows = tokens.shape[0]
    each = rows // (groups * gx)
    held = rows // (groups * gy)
    m = lax.broadcasted_iota(jnp.int32, (rows, rows), 0)
    source = lax.broadcasted_iota(jnp.int32, (rows, rows), 1)
    j, q, i = m // (groups * each), (m // each) % groups, m % each
    mine, other = masks(gx, 0), masks(gx, 1)
    flip = jnp.zeros_like(j)
    for n in range(len(mine)):
        bit = (j // (1 << (len(mine) - 1 - n))) % 2
        flip = flip + bit * jnp.where(core == 0, mine[n], other[n])
    row = (x ^ flip) * each + i
    wanted = (q * gy + (row // held + gy - core) % gy) * held + row % held
    pick = (source == wanted).astype(jnp.bfloat16)
    return jnp.dot(pick, tokens, preferred_element_type=jnp.float32).astype(jnp.bfloat16)


def project_kernel(sizes, all_blocks, block, tokens_ref, ahead_ref, gate_hbm, up_hbm, send_ref, keep_ref, rows_ref, buffer, sems):
    base = lax.axis_index("groups") * all_blocks
    slots = buffer.shape[0]
    ahead = ahead_ref.shape[0]
    later = all_blocks - ahead

    def copies(i, slot):
        return weight_copies((gate_hbm, up_hbm), buffer.at[slot], sems.at[slot], base + ahead + i, block)

    for i in range(min(slots - 1, later)):
        for copy in copies(i, i):
            copy.start()

    rows_ref[...] = pick_rows(sizes, tokens_ref[...])
    half = rows_ref.shape[0] // 2

    def multiply(n, w, weights):
        columns = pl.ds(n * block if isinstance(n, int) else pl.multiple_of(n * block, LANES), block)
        total = jnp.dot(rows_ref[...], weights, preferred_element_type=jnp.float32)
        keep_ref[w, :, columns] = total[:half]
        send_ref[w, :, columns] = total[half:]

    for n in range(ahead):
        for w in range(2):
            multiply(n, w, ahead_ref[n, w])

    def step(n, carry):
        slot = lax.rem(n, slots)

        @pl.when(n + slots - 1 < later)
        def _():
            for copy in copies(n + slots - 1, lax.rem(n + slots - 1, slots)):
                copy.start()

        for w, copy in enumerate(copies(n, slot)):
            copy.wait()
            multiply(ahead + n, w, buffer[slot, w])
        return carry

    lax.fori_loop(0, later, step, 0)


def project(sizes, all_blocks, block, tokens, ahead, gate_weight, up_weight):
    rows, depth = tokens.shape
    width = all_blocks * block
    slots = 4
    shape = jax.ShapeDtypeStruct((2, rows // 2, width), jnp.float32)
    return pl.pallas_call(
        functools.partial(project_kernel, sizes, all_blocks, block),
        in_specs=[pl.BlockSpec(memory_space=pltpu.VMEM)] * 2 + [pl.BlockSpec(memory_space=pl.ANY)] * 2,
        out_specs=[pl.BlockSpec(memory_space=pltpu.VMEM)] * 2,
        out_shape=[shape, shape],
        scratch_shapes=[
            pltpu.VMEM((rows, depth), jnp.bfloat16),
            pltpu.VMEM((slots, 2, depth, block), jnp.bfloat16),
            pltpu.SemaphoreType.DMA((slots, 2)),
        ],
        cost_estimate=pl.CostEstimate(
            flops=4 * rows * depth * width, bytes_accessed=4 * depth * width, transcendentals=0
        ),
        compiler_params=pltpu.CompilerParams(vmem_limit_bytes=32 << 20),
    )(tokens, ahead, gate_weight, up_weight)


def gather_rows(sizes, tokens):
    groups, gx, gy = sizes
    both = [
        (g * gy + core, (g + 1) % groups * gy + (core + 1) % gy) for g in range(groups) for core in range(gy)
    ]
    across = lax.ppermute(tokens, "groups", [(g, (g + 1) % groups) for g in range(groups)])
    diagonal = lax.ppermute(tokens, ("groups", "gy"), both)
    beside = lax.ppermute(tokens, "gy", [(core, (core + 1) % gy) for core in range(gy)])
    return jnp.concatenate([tokens, beside, across, diagonal], axis=0)


def per_device(sizes, tokens, gate_weight, up_weight):
    groups, gx, gy = sizes
    width = gate_weight.shape[1] // groups
    block = column_block(width)
    all_blocks = width // block
    ahead = fetch(all_blocks, block, min(3, all_blocks), gate_weight, up_weight)
    rows = gather_rows(sizes, tokens)
    send, keep = project(sizes, all_blocks, block, rows, ahead, gate_weight, up_weight)
    phases = gx.bit_length() - 1
    for n in range(phases):
        pairs = [
            (x * gy + core, (x ^ masks(gx, core)[n]) * gy + core) for x in range(gx) for core in range(gy)
        ]
        total = keep + lax.ppermute(send, ("gx", "gy"), pairs)
        half = total.shape[1] // 2
        if n < phases - 1:
            keep, send = total[:, :half], total[:, half:]
    hidden = (jax.nn.silu(total[0]) * total[1]).astype(jnp.bfloat16)
    each = hidden.shape[0] // groups
    own, theirs = hidden[:each], hidden[each:]
    theirs = lax.ppermute(theirs, "groups", [(g, (g + 1) % groups) for g in range(groups)])
    first = lax.axis_index("groups") == 0
    return jnp.concatenate([jnp.where(first, own, theirs), jnp.where(first, theirs, own)], axis=1)


def solution(mesh):
    sizes = tuple(mesh.shape[name] for name in ("groups", "gx", "gy"))
    in_specs = (P(("groups", "gy"), "gx"), P("gx", "gy"), P("gx", "gy"))
    out_specs = P(("groups", "gx"), "gy")
    return jax.shard_map(
        functools.partial(per_device, sizes), mesh=mesh, in_specs=in_specs, out_specs=out_specs, check_vma=False
    )
```

```python
import functools

import jax
import jax.numpy as jnp
from jax import lax
from jax.experimental import pallas as pl
from jax.experimental.pallas import tpu as pltpu
from jax.sharding import PartitionSpec as P

LANES = 128
POWER = 64
FLOOR = 2.0 ** (-120.0 / POWER)
SCALE = 2.0 ** (120.0 / POWER) - FLOOR
LEAST = 2.0**-100


def encode(y, bound):
    code = jnp.abs(y) * (SCALE / bound) + FLOOR
    for _ in range(POWER.bit_length() - 1):
        code = code * code
    return jnp.where(y < 0, -code, code).astype(jnp.bfloat16)


def decode(code, bound):
    code = code.astype(jnp.float32)
    y = (jnp.exp(jnp.log(jnp.abs(code)) * (1.0 / POWER)) - FLOOR) * (bound * (1.0 / SCALE))
    return jnp.where(code < 0, -y, y)


def rounded_up(bound):
    return lax.reduce_precision(jnp.maximum(bound * (1.0 + 2.0**-6), LEAST), 8, 7)


def masks(count, core):
    bits = [1 << b for b in range(count.bit_length() - 1)]
    if core % 2 and len(bits) > 1:
        bits[0], bits[1] = bits[1], bits[0]
    return bits


def column_block(width):
    units = width // LANES
    return LANES * max(d for d in range(1, min(units, 4) + 1) if units % d == 0)


def weight_copies(weights, target, sems, column, block):
    columns = pl.ds(pl.multiple_of(column * block, LANES), block)
    return [pltpu.make_async_copy(w.at[:, columns], target.at[i], sems.at[i]) for i, w in enumerate(weights)]


def fetch_kernel(all_blocks, block, gate_hbm, up_hbm, ahead_ref, sems):
    base = lax.axis_index("groups") * all_blocks
    copies = []
    for n in range(ahead_ref.shape[0]):
        copies += weight_copies((gate_hbm, up_hbm), ahead_ref.at[n], sems.at[n], base + n, block)
    for copy in copies:
        copy.start()
    for copy in copies:
        copy.wait()


def fetch(all_blocks, block, ahead, gate_weight, up_weight):
    depth = gate_weight.shape[0]
    return pl.pallas_call(
        functools.partial(fetch_kernel, all_blocks, block),
        in_specs=[pl.BlockSpec(memory_space=pl.ANY)] * 2,
        out_specs=pl.BlockSpec(memory_space=pltpu.VMEM),
        out_shape=jax.ShapeDtypeStruct((ahead, 2, depth, block), jnp.bfloat16),
        scratch_shapes=[pltpu.SemaphoreType.DMA((ahead, 2))],
        cost_estimate=pl.CostEstimate(flops=0, bytes_accessed=4 * depth * ahead * block, transcendentals=0),
        compiler_params=pltpu.CompilerParams(vmem_limit_bytes=16 << 20),
    )(gate_weight, up_weight)


def pick_rows(sizes, tokens):
    groups, gx, gy = sizes
    group, x, core = lax.axis_index("groups"), lax.axis_index("gx"), lax.axis_index("gy")
    rows = tokens.shape[0]
    each = rows // (groups * gx)
    held = rows // (groups * gy)
    m = lax.broadcasted_iota(jnp.int32, (rows, rows), 0)
    source = lax.broadcasted_iota(jnp.int32, (rows, rows), 1)
    j, q, i = m // (groups * each), (m // each) % groups, m % each
    mine, other = masks(gx, 0), masks(gx, 1)
    flip = jnp.zeros_like(j)
    for n in range(len(mine)):
        bit = (j // (1 << (len(mine) - 1 - n))) % 2
        flip = flip + bit * jnp.where(core == 0, mine[n], other[n])
    row = (x ^ flip) * each + i
    wanted = (q * gy + (row // held + gy - core) % gy) * held + row % held
    pick = (source == wanted).astype(jnp.bfloat16)
    return jnp.dot(pick, tokens, preferred_element_type=jnp.float32).astype(jnp.bfloat16)


def project_kernel(sizes, all_blocks, block, tokens_ref, ahead_ref, gate_hbm, up_hbm, send_ref, keep_ref, rows_ref, half_ref, buffer, sems):
    base = lax.axis_index("groups") * all_blocks
    slots = buffer.shape[0]
    ahead = ahead_ref.shape[0]
    later = all_blocks - ahead

    def copies(i, slot):
        return weight_copies((gate_hbm, up_hbm), buffer.at[slot], sems.at[slot], base + ahead + i, block)

    for i in range(min(slots - 1, later)):
        for copy in copies(i, i):
            copy.start()

    rows_ref[...] = pick_rows(sizes, tokens_ref[...])
    half = rows_ref.shape[0] // 2

    tiles = block // LANES

    def multiply(n, w, weights):
        total = jnp.dot(rows_ref[...], weights, preferred_element_type=jnp.float32)
        for t in range(tiles):
            tile = total[:, t * LANES : (t + 1) * LANES]
            keep_ref[w, n * tiles + t] = tile[:half]
            half_ref[w, n * tiles + t] = tile[half:]

    for n in range(ahead):
        for w in range(2):
            multiply(n, w, ahead_ref[n, w])

    def step(n, carry):
        slot = lax.rem(n, slots)

        @pl.when(n + slots - 1 < later)
        def _():
            for copy in copies(n + slots - 1, lax.rem(n + slots - 1, slots)):
                copy.start()

        for w, copy in enumerate(copies(n, slot)):
            copy.wait()
            multiply(ahead + n, w, buffer[slot, w])
        return carry

    lax.fori_loop(0, later, step, 0)

    every = all_blocks * tiles
    def bound_of(ref, w):
        peak = jnp.zeros((half, LANES), jnp.float32)
        for n in range(all_blocks):
            peak = jnp.maximum(peak, jnp.max(jnp.abs(ref[w, n * tiles : (n + 1) * tiles]), axis=0))
        peak = jnp.broadcast_to(jnp.max(peak, axis=1, keepdims=True), (half, LANES))
        return jnp.maximum(peak * (1.0 + 2.0**-6), LEAST).astype(jnp.bfloat16)

    for w in range(2):
        keep_ref[w, every] = bound_of(keep_ref, w).astype(jnp.float32)
        bound = bound_of(half_ref, w)
        send_ref[w, every] = bound
        bound = bound.astype(jnp.float32)
        for n in range(all_blocks):
            now = slice(n * tiles, (n + 1) * tiles)
            send_ref[w, now] = encode(half_ref[w, now], bound[None])


def project(sizes, all_blocks, block, tokens, ahead, gate_weight, up_weight):
    rows, depth = tokens.shape
    width = all_blocks * block
    slots = 4
    half = rows // 2
    return pl.pallas_call(
        functools.partial(project_kernel, sizes, all_blocks, block),
        in_specs=[pl.BlockSpec(memory_space=pltpu.VMEM)] * 2 + [pl.BlockSpec(memory_space=pl.ANY)] * 2,
        out_specs=[pl.BlockSpec(memory_space=pltpu.VMEM)] * 2,
        out_shape=[
            jax.ShapeDtypeStruct((2, width // LANES + 1, half, LANES), jnp.bfloat16),
            jax.ShapeDtypeStruct((2, width // LANES + 1, half, LANES), jnp.float32),
        ],
        scratch_shapes=[
            pltpu.VMEM((rows, depth), jnp.bfloat16),
            pltpu.VMEM((2, width // LANES, half, LANES), jnp.float32),
            pltpu.VMEM((slots, 2, depth, block), jnp.bfloat16),
            pltpu.SemaphoreType.DMA((slots, 2)),
        ],
        cost_estimate=pl.CostEstimate(
            flops=4 * rows * depth * width, bytes_accessed=4 * depth * width, transcendentals=0
        ),
        compiler_params=pltpu.CompilerParams(vmem_limit_bytes=32 << 20),
    )(tokens, ahead, gate_weight, up_weight)


def gather_rows(sizes, tokens):
    groups, gx, gy = sizes
    both = [
        (g * gy + core, (g + 1) % groups * gy + (core + 1) % gy) for g in range(groups) for core in range(gy)
    ]
    across = lax.ppermute(tokens, "groups", [(g, (g + 1) % groups) for g in range(groups)])
    diagonal = lax.ppermute(tokens, ("groups", "gy"), both)
    beside = lax.ppermute(tokens, "gy", [(core, (core + 1) % gy) for core in range(gy)])
    return jnp.concatenate([tokens, beside, across, diagonal], axis=0)


def per_device(sizes, tokens, gate_weight, up_weight):
    groups, gx, gy = sizes
    width = gate_weight.shape[1] // groups
    block = column_block(width)
    all_blocks = width // block
    ahead = fetch(all_blocks, block, min(3, all_blocks), gate_weight, up_weight)
    rows = gather_rows(sizes, tokens)
    send, keep = project(sizes, all_blocks, block, rows, ahead, gate_weight, up_weight)
    keep, bound = keep[:, :-1], keep[:, -1:]
    phases = gx.bit_length() - 1
    for n in range(phases):
        pairs = [
            (x * gy + core, (x ^ masks(gx, core)[n]) * gy + core) for x in range(gx) for core in range(gy)
        ]
        came = lax.ppermute(send, ("gx", "gy"), pairs)
        came, came_bound = came[:, :-1], came[:, -1:].astype(jnp.float32)
        total = keep + decode(came, came_bound)
        half = total.shape[2] // 2
        if n < phases - 1:
            bound = rounded_up(bound + came_bound)
            send = encode(total[:, :, half:], bound[:, :, half:])
            send = jnp.concatenate([send, bound[:, :, half:].astype(jnp.bfloat16)], axis=1)
            keep, bound = total[:, :, :half], bound[:, :, :half]
    hidden = (jax.nn.silu(total[0]) * total[1]).astype(jnp.bfloat16)
    hidden = jnp.swapaxes(hidden, 0, 1).reshape(hidden.shape[1], width)
    each = hidden.shape[0] // groups
    own, theirs = hidden[:each], hidden[each:]
    theirs = lax.ppermute(theirs, "groups", [(g, (g + 1) % groups) for g in range(groups)])
    first = lax.axis_index("groups") == 0
    return jnp.concatenate([jnp.where(first, own, theirs), jnp.where(first, theirs, own)], axis=1)


def solution(mesh):
    sizes = tuple(mesh.shape[name] for name in ("groups", "gx", "gy"))
    in_specs = (P(("groups", "gy"), "gx"), P("gx", "gy"), P("gx", "gy"))
    out_specs = P(("groups", "gx"), "gy")
    return jax.shard_map(
        functools.partial(per_device, sizes), mesh=mesh, in_specs=in_specs, out_specs=out_specs, check_vma=False
    )
```

```python
import functools

import jax
import jax.numpy as jnp
from jax import lax
from jax.experimental import pallas as pl
from jax.experimental.pallas import tpu as pltpu
from jax.sharding import PartitionSpec as P

LANES = 128
POWER = 64
FLOOR = 2.0 ** (-120.0 / POWER)
SCALE = 2.0 ** (120.0 / POWER) - FLOOR
LEAST = 2.0**-100


def encode(y, bound):
    code = jnp.abs(y) * (SCALE / bound) + FLOOR
    for _ in range(POWER.bit_length() - 1):
        code = code * code
    return jnp.where(y < 0, -code, code).astype(jnp.bfloat16)


def decode(code, bound):
    code = code.astype(jnp.float32)
    y = (jnp.exp(jnp.log(jnp.abs(code)) * (1.0 / POWER)) - FLOOR) * (bound * (1.0 / SCALE))
    return jnp.where(code < 0, -y, y)


def rounded_up(bound):
    return lax.reduce_precision(jnp.maximum(bound * (1.0 + 2.0**-6), LEAST), 8, 7)


def masks(count, core):
    bits = [1 << b for b in range(count.bit_length() - 1)]
    if core % 2 and len(bits) > 1:
        bits[0], bits[1] = bits[1], bits[0]
    return bits


def column_block(width):
    units = width // LANES
    return LANES * max(d for d in range(1, min(units, 4) + 1) if units % d == 0)


def weight_copies(weights, target, sems, column, block):
    columns = pl.ds(pl.multiple_of(column * block, LANES), block)
    return [pltpu.make_async_copy(w.at[:, columns], target.at[i], sems.at[i]) for i, w in enumerate(weights)]


def fetch_kernel(all_blocks, block, gate_hbm, up_hbm, ahead_ref, sems):
    base = lax.axis_index("groups") * all_blocks
    copies = []
    for n in range(ahead_ref.shape[0]):
        copies += weight_copies((gate_hbm, up_hbm), ahead_ref.at[n], sems.at[n], base + n, block)
    for copy in copies:
        copy.start()
    for copy in copies:
        copy.wait()


def fetch(all_blocks, block, ahead, gate_weight, up_weight):
    depth = gate_weight.shape[0]
    return pl.pallas_call(
        functools.partial(fetch_kernel, all_blocks, block),
        in_specs=[pl.BlockSpec(memory_space=pl.ANY)] * 2,
        out_specs=pl.BlockSpec(memory_space=pltpu.VMEM),
        out_shape=jax.ShapeDtypeStruct((ahead, 2, depth, block), jnp.bfloat16),
        scratch_shapes=[pltpu.SemaphoreType.DMA((ahead, 2))],
        cost_estimate=pl.CostEstimate(flops=0, bytes_accessed=4 * depth * ahead * block, transcendentals=0),
        compiler_params=pltpu.CompilerParams(vmem_limit_bytes=16 << 20),
    )(gate_weight, up_weight)


def pick_rows(sizes, tokens, w):
    groups, gx, gy = sizes
    group, x, core = lax.axis_index("groups"), lax.axis_index("gx"), lax.axis_index("gy")
    rows = tokens.shape[0]
    each = rows // (groups * gx)
    held = rows // (groups * gy)
    quarter = rows // 4
    place = lax.broadcasted_iota(jnp.int32, (rows, rows), 0)
    source = lax.broadcasted_iota(jnp.int32, (rows, rows), 1)
    m = (place // quarter ^ w) * quarter + place % quarter
    j, q, i = m // (groups * each), (m // each) % groups, m % each
    mine, other = masks(gx, 0), masks(gx, 1)
    flip = jnp.zeros_like(j)
    for n in range(len(mine)):
        bit = (j // (1 << (len(mine) - 1 - n))) % 2
        flip = flip + bit * jnp.where(core == 0, mine[n], other[n])
    row = (x ^ flip) * each + i
    wanted = (q * gy + (row // held + gy - core) % gy) * held + row % held
    pick = (source == wanted).astype(jnp.bfloat16)
    return jnp.dot(pick, tokens, preferred_element_type=jnp.float32).astype(jnp.bfloat16)


def project_kernel(
    sizes, all_blocks, block, tokens_ref, ahead_ref, gate_hbm, up_hbm, keep_ref, *refs
):
    *send_refs, rows_ref, total_ref, buffer, sems = refs
    base = lax.axis_index("groups") * all_blocks
    slots = buffer.shape[0]
    ahead = ahead_ref.shape[0]
    later = all_blocks - ahead

    def copies(i, slot):
        return weight_copies((gate_hbm, up_hbm), buffer.at[slot], sems.at[slot], base + ahead + i, block)

    for i in range(min(slots - 1, later)):
        for copy in copies(i, i):
            copy.start()

    for w in range(2):
        rows_ref[w] = pick_rows(sizes, tokens_ref[...], w)
    high = total_ref.shape[3]
    tiles = block // LANES

    def multiply(n, w, weights):
        product = jnp.dot(rows_ref[w], weights, preferred_element_type=jnp.float32)
        for h in range(2):
            for t in range(tiles):
                total_ref[w, h, n * tiles + t] = product[h * high : (h + 1) * high, t * LANES : (t + 1) * LANES]

    for n in range(ahead):
        for w in range(2):
            multiply(n, w, ahead_ref[n, w])

    def step(n, carry):
        slot = lax.rem(n, slots)

        @pl.when(n + slots - 1 < later)
        def _():
            for copy in copies(n + slots - 1, lax.rem(n + slots - 1, slots)):
                copy.start()

        for w, copy in enumerate(copies(n, slot)):
            copy.wait()
            multiply(ahead + n, w, buffer[slot, w])
        return carry

    lax.fori_loop(0, later, step, 0)

    every = all_blocks * tiles
    spans = [slice(n * tiles, (n + 1) * tiles) for n in range(all_blocks)]
    first = lax.broadcasted_iota(jnp.int32, (tiles, high, LANES), 1) < high // 2
    for h in range(2):
        peaks = [jnp.zeros((high, LANES), jnp.float32)] * 2
        for span in spans:
            gate, up = total_ref[0, h, span], total_ref[1, h, span]
            parts = jnp.where(first, gate, up), pltpu.roll(jnp.where(first, up, gate), high // 2, 1)
            for i, part in enumerate(parts):
                total_ref[i, h, span] = part
                peaks[i] = jnp.maximum(peaks[i], jnp.max(jnp.abs(part), axis=0))
        for i in range(2):
            peak = jnp.broadcast_to(jnp.max(peaks[i], axis=1, keepdims=True), (high, LANES))
            bound = jnp.maximum(peak * (1.0 + 2.0**-6), LEAST).astype(jnp.bfloat16)
            exact = bound.astype(jnp.float32)
            if h == i == 0:
                keep_ref[every] = exact
                for span in spans:
                    keep_ref[span] = total_ref[i, h, span]
                continue
            send_ref = send_refs[2 * h + i - 1]
            send_ref[every] = bound
            for span in spans:
                send_ref[span] = encode(total_ref[i, h, span], exact[None])


def project(sizes, all_blocks, block, tokens, ahead, gate_weight, up_weight):
    rows, depth = tokens.shape
    width = all_blocks * block
    slots = 4
    shape = (width // LANES + 1, rows // 2, LANES)
    return pl.pallas_call(
        functools.partial(project_kernel, sizes, all_blocks, block),
        in_specs=[pl.BlockSpec(memory_space=pltpu.VMEM)] * 2 + [pl.BlockSpec(memory_space=pl.ANY)] * 2,
        out_specs=[pl.BlockSpec(memory_space=pltpu.VMEM)] * 4,
        out_shape=[jax.ShapeDtypeStruct(shape, jnp.float32)] + [jax.ShapeDtypeStruct(shape, jnp.bfloat16)] * 3,
        scratch_shapes=[
            pltpu.VMEM((2, rows, depth), jnp.bfloat16),
            pltpu.VMEM((2, 2, width // LANES, rows // 2, LANES), jnp.float32),
            pltpu.VMEM((slots, 2, depth, block), jnp.bfloat16),
            pltpu.SemaphoreType.DMA((slots, 2)),
        ],
        cost_estimate=pl.CostEstimate(
            flops=4 * rows * depth * width, bytes_accessed=4 * depth * width, transcendentals=0
        ),
        compiler_params=pltpu.CompilerParams(vmem_limit_bytes=32 << 20),
    )(tokens, ahead, gate_weight, up_weight)


def exchange(sizes, send, flip):
    groups, gx, gy = sizes
    pairs = [(x * gy + core, (x ^ flip(core)) * gy + core) for x in range(gx) for core in range(gy)]
    return lax.ppermute(send, ("gx", "gy"), pairs)


def opened(came):
    bound = came[-1:].astype(jnp.float32)
    return decode(came[:-1], bound), bound


def gather_rows(sizes, tokens):
    groups, gx, gy = sizes
    both = [
        (g * gy + core, (g + 1) % groups * gy + (core + 1) % gy) for g in range(groups) for core in range(gy)
    ]
    across = lax.ppermute(tokens, "groups", [(g, (g + 1) % groups) for g in range(groups)])
    diagonal = lax.ppermute(tokens, ("groups", "gy"), both)
    beside = lax.ppermute(tokens, "gy", [(core, (core + 1) % gy) for core in range(gy)])
    return jnp.concatenate([tokens, beside, across, diagonal], axis=0)


def per_device(sizes, tokens, gate_weight, up_weight):
    groups, gx, gy = sizes
    width = gate_weight.shape[1] // groups
    block = column_block(width)
    all_blocks = width // block
    ahead = fetch(all_blocks, block, min(3, all_blocks), gate_weight, up_weight)
    rows = gather_rows(sizes, tokens)
    keep, *sends = project(sizes, all_blocks, block, rows, ahead, gate_weight, up_weight)
    flips = [
        lambda core: masks(gx, core)[1],
        lambda core: masks(gx, core)[0],
        lambda core: masks(gx, core)[0] ^ masks(gx, core)[1],
    ]
    came = lax.optimization_barrier([exchange(sizes, send, flip) for send, flip in zip(sends, flips)])
    total, bound = keep[:-1], keep[-1:]
    for part in came:
        value, part_bound = opened(part)
        total, bound = total + value, bound + part_bound
    shape = (2, total.shape[1] // 2, LANES)
    total, bound = total.reshape(-1, *shape), bound.reshape(-1, *shape)
    for n in range(2, gx.bit_length() - 1):
        half = total.shape[2] // 2
        bound = rounded_up(bound)
        send = encode(total[:, :, half:], bound[:, :, half:])
        send = jnp.concatenate([send, bound[:, :, half:].astype(jnp.bfloat16)], axis=0)
        value, part_bound = opened(exchange(sizes, send, lambda core: masks(gx, core)[n]))
        total, bound = total[:, :, :half] + value, bound[:, :, :half] + part_bound
    hidden = (jax.nn.silu(total[:, 0]) * total[:, 1]).astype(jnp.bfloat16)
    hidden = jnp.swapaxes(hidden, 0, 1).reshape(hidden.shape[1], width)
    each = hidden.shape[0] // groups
    own, theirs = hidden[:each], hidden[each:]
    theirs = lax.ppermute(theirs, "groups", [(g, (g + 1) % groups) for g in range(groups)])
    first = lax.axis_index("groups") == 0
    return jnp.concatenate([jnp.where(first, own, theirs), jnp.where(first, theirs, own)], axis=1)


def solution(mesh):
    sizes = tuple(mesh.shape[name] for name in ("groups", "gx", "gy"))
    in_specs = (P(("groups", "gy"), "gx"), P("gx", "gy"), P("gx", "gy"))
    out_specs = P(("groups", "gx"), "gy")
    return jax.shard_map(
        functools.partial(per_device, sizes), mesh=mesh, in_specs=in_specs, out_specs=out_specs, check_vma=False
    )
```

```python
import functools

import jax
import jax.numpy as jnp
from jax import lax
from jax.experimental import pallas as pl
from jax.experimental.pallas import tpu as pltpu
from jax.sharding import PartitionSpec as P

LANES = 128
POWER = 64
FLOOR = 2.0 ** (-120.0 / POWER)
SCALE = 2.0 ** (120.0 / POWER) - FLOOR
LEAST = 2.0**-100


def encode(y, bound):
    code = jnp.abs(y) * (SCALE / bound) + FLOOR
    for _ in range(POWER.bit_length() - 1):
        code = code * code
    return jnp.where(y < 0, -code, code).astype(jnp.bfloat16)


def decode(code, bound):
    code = code.astype(jnp.float32)
    y = (jnp.exp(jnp.log(jnp.abs(code)) * (1.0 / POWER)) - FLOOR) * (bound * (1.0 / SCALE))
    return jnp.where(code < 0, -y, y)


def rounded_up(bound):
    return lax.reduce_precision(jnp.maximum(bound * (1.0 + 2.0**-6), LEAST), 8, 7)


def flips(core):
    return (0, 2, 1, 3) if core % 2 else (0, 3, 2, 1)


def column_block(width):
    units = width // LANES
    return LANES * max(d for d in range(1, min(units, 4) + 1) if units % d == 0)


def weight_copies(weights, target, sems, column, block):
    columns = pl.ds(pl.multiple_of(column * block, LANES), block)
    return [pltpu.make_async_copy(w.at[:, columns], target.at[i], sems.at[i]) for i, w in enumerate(weights)]


def fetch_kernel(all_blocks, block, gate_hbm, up_hbm, ahead_ref, sems):
    base = lax.axis_index("groups") * all_blocks
    copies = []
    for n in range(ahead_ref.shape[0]):
        copies += weight_copies((gate_hbm, up_hbm), ahead_ref.at[n], sems.at[n], base + n, block)
    for copy in copies:
        copy.start()
    for copy in copies:
        copy.wait()


def fetch(all_blocks, block, ahead, gate_weight, up_weight):
    depth = gate_weight.shape[0]
    return pl.pallas_call(
        functools.partial(fetch_kernel, all_blocks, block),
        in_specs=[pl.BlockSpec(memory_space=pl.ANY)] * 2,
        out_specs=pl.BlockSpec(memory_space=pltpu.VMEM),
        out_shape=jax.ShapeDtypeStruct((ahead, 2, depth, block), jnp.bfloat16),
        scratch_shapes=[pltpu.SemaphoreType.DMA((ahead, 2))],
        cost_estimate=pl.CostEstimate(flops=0, bytes_accessed=4 * depth * ahead * block, transcendentals=0),
        compiler_params=pltpu.CompilerParams(vmem_limit_bytes=16 << 20),
    )(gate_weight, up_weight)


def pick_rows(sizes, tokens, w):
    groups, gx, gy = sizes
    group, x, core = lax.axis_index("groups"), lax.axis_index("gx"), lax.axis_index("gy")
    rows = tokens.shape[0]
    each = rows // (groups * gx)
    held = rows // (groups * gy)
    quarter = rows // 4
    place = lax.broadcasted_iota(jnp.int32, (rows, rows), 0)
    source = lax.broadcasted_iota(jnp.int32, (rows, rows), 1)
    m = (place // quarter ^ w) * quarter + place % quarter
    j, q, i = m // (groups * each), (m // each) % groups, m % each
    steps = gx // 4
    part, flip = j // steps, jnp.zeros_like(j)
    for n in range(1, 4):
        flip = flip + jnp.where(part == n, jnp.where(core == 0, flips(0)[n], flips(1)[n]), 0)
    for n in range(2, gx.bit_length() - 1):
        steps //= 2
        flip = flip + j // steps % 2 * (1 << n)
    row = (x ^ flip) * each + i
    wanted = (q * gy + (row // held + gy - core) % gy) * held + row % held
    pick = (source == wanted).astype(jnp.bfloat16)
    return jnp.dot(pick, tokens, preferred_element_type=jnp.float32).astype(jnp.bfloat16)


def project_kernel(
    sizes, all_blocks, block, tokens_ref, ahead_ref, gate_hbm, up_hbm, keep_ref, *refs
):
    *send_refs, rows_ref, total_ref, buffer, sems = refs
    base = lax.axis_index("groups") * all_blocks
    slots = buffer.shape[0]
    ahead = ahead_ref.shape[0]
    later = all_blocks - ahead

    def copies(i, slot):
        return weight_copies((gate_hbm, up_hbm), buffer.at[slot], sems.at[slot], base + ahead + i, block)

    for i in range(min(slots - 1, later)):
        for copy in copies(i, i):
            copy.start()

    for w in range(2):
        rows_ref[w] = pick_rows(sizes, tokens_ref[...], w)
    high = total_ref.shape[3]
    tiles = block // LANES

    def multiply(n, w, weights):
        product = jnp.dot(rows_ref[w], weights, preferred_element_type=jnp.float32)
        for h in range(2):
            for t in range(tiles):
                total_ref[w, h, n * tiles + t] = product[h * high : (h + 1) * high, t * LANES : (t + 1) * LANES]

    for n in range(ahead):
        for w in range(2):
            multiply(n, w, ahead_ref[n, w])

    def step(n, carry):
        slot = lax.rem(n, slots)

        @pl.when(n + slots - 1 < later)
        def _():
            for copy in copies(n + slots - 1, lax.rem(n + slots - 1, slots)):
                copy.start()

        for w, copy in enumerate(copies(n, slot)):
            copy.wait()
            multiply(ahead + n, w, buffer[slot, w])
        return carry

    lax.fori_loop(0, later, step, 0)

    every = all_blocks * tiles
    spans = [slice(n * tiles, (n + 1) * tiles) for n in range(all_blocks)]
    first = lax.broadcasted_iota(jnp.int32, (tiles, high, LANES), 1) < high // 2
    for h in range(2):
        peaks = [jnp.zeros((high, LANES), jnp.float32)] * 2
        for span in spans:
            gate, up = total_ref[0, h, span], total_ref[1, h, span]
            parts = jnp.where(first, gate, up), pltpu.roll(jnp.where(first, up, gate), high // 2, 1)
            for i, part in enumerate(parts):
                total_ref[i, h, span] = part
                peaks[i] = jnp.maximum(peaks[i], jnp.max(jnp.abs(part), axis=0))
        for i in range(2):
            peak = jnp.broadcast_to(jnp.max(peaks[i], axis=1, keepdims=True), (high, LANES))
            bound = jnp.maximum(peak * (1.0 + 2.0**-6), LEAST).astype(jnp.bfloat16)
            exact = bound.astype(jnp.float32)
            if h == i == 0:
                keep_ref[every] = exact
                for span in spans:
                    keep_ref[span] = total_ref[i, h, span]
                continue
            send_ref = send_refs[2 * h + i - 1]
            send_ref[every] = bound
            for span in spans:
                send_ref[span] = encode(total_ref[i, h, span], exact[None])


def project(sizes, all_blocks, block, tokens, ahead, gate_weight, up_weight):
    rows, depth = tokens.shape
    width = all_blocks * block
    slots = 4
    shape = (width // LANES + 1, rows // 2, LANES)
    return pl.pallas_call(
        functools.partial(project_kernel, sizes, all_blocks, block),
        in_specs=[pl.BlockSpec(memory_space=pltpu.VMEM)] * 2 + [pl.BlockSpec(memory_space=pl.ANY)] * 2,
        out_specs=[pl.BlockSpec(memory_space=pltpu.VMEM)] * 4,
        out_shape=[jax.ShapeDtypeStruct(shape, jnp.float32)] + [jax.ShapeDtypeStruct(shape, jnp.bfloat16)] * 3,
        scratch_shapes=[
            pltpu.VMEM((2, rows, depth), jnp.bfloat16),
            pltpu.VMEM((2, 2, width // LANES, rows // 2, LANES), jnp.float32),
            pltpu.VMEM((slots, 2, depth, block), jnp.bfloat16),
            pltpu.SemaphoreType.DMA((slots, 2)),
        ],
        cost_estimate=pl.CostEstimate(
            flops=4 * rows * depth * width, bytes_accessed=4 * depth * width, transcendentals=0
        ),
        compiler_params=pltpu.CompilerParams(vmem_limit_bytes=32 << 20),
    )(tokens, ahead, gate_weight, up_weight)


def exchange(sizes, send, flip):
    groups, gx, gy = sizes
    pairs = [(x * gy + core, (x ^ flip(core)) * gy + core) for x in range(gx) for core in range(gy)]
    return lax.ppermute(send, ("gx", "gy"), pairs)


def opened(came):
    bound = came[-1:].astype(jnp.float32)
    return decode(came[:-1], bound), bound


def gather_rows(sizes, tokens):
    groups, gx, gy = sizes
    both = [
        (g * gy + core, (g + 1) % groups * gy + (core + 1) % gy) for g in range(groups) for core in range(gy)
    ]
    across = lax.ppermute(tokens, "groups", [(g, (g + 1) % groups) for g in range(groups)])
    diagonal = lax.ppermute(tokens, ("groups", "gy"), both)
    beside = lax.ppermute(tokens, "gy", [(core, (core + 1) % gy) for core in range(gy)])
    return jnp.concatenate([tokens, beside, across, diagonal], axis=0)


def per_device(sizes, tokens, gate_weight, up_weight):
    groups, gx, gy = sizes
    width = gate_weight.shape[1] // groups
    block = column_block(width)
    all_blocks = width // block
    ahead = fetch(all_blocks, block, min(3, all_blocks), gate_weight, up_weight)
    rows = gather_rows(sizes, tokens)
    keep, *sends = project(sizes, all_blocks, block, rows, ahead, gate_weight, up_weight)
    came = [exchange(sizes, send, lambda core: flips(core)[n + 1]) for n, send in enumerate(sends)]
    came = lax.optimization_barrier(came)
    total, bound = keep[:-1], keep[-1:]
    for part in came:
        value, part_bound = opened(part)
        total, bound = total + value, bound + part_bound
    shape = (2, total.shape[1] // 2, LANES)
    total, bound = total.reshape(-1, *shape), bound.reshape(-1, *shape)
    for n in range(2, gx.bit_length() - 1):
        half = total.shape[2] // 2
        bound = rounded_up(bound)
        send = encode(total[:, :, half:], bound[:, :, half:])
        send = jnp.concatenate([send, bound[:, :, half:].astype(jnp.bfloat16)], axis=0)
        value, part_bound = opened(exchange(sizes, send, lambda core: 1 << n))
        total, bound = total[:, :, :half] + value, bound[:, :, :half] + part_bound
    hidden = (jax.nn.silu(total[:, 0]) * total[:, 1]).astype(jnp.bfloat16)
    hidden = jnp.swapaxes(hidden, 0, 1).reshape(hidden.shape[1], width)
    each = hidden.shape[0] // groups
    own, theirs = hidden[:each], hidden[each:]
    theirs = lax.ppermute(theirs, "groups", [(g, (g + 1) % groups) for g in range(groups)])
    first = lax.axis_index("groups") == 0
    return jnp.concatenate([jnp.where(first, own, theirs), jnp.where(first, theirs, own)], axis=1)


def solution(mesh):
    sizes = tuple(mesh.shape[name] for name in ("groups", "gx", "gy"))
    in_specs = (P(("groups", "gy"), "gx"), P("gx", "gy"), P("gx", "gy"))
    out_specs = P(("groups", "gx"), "gy")
    return jax.shard_map(
        functools.partial(per_device, sizes), mesh=mesh, in_specs=in_specs, out_specs=out_specs, check_vma=False
    )
```

```python
import functools

import jax
import jax.numpy as jnp
from jax import lax
from jax.experimental import pallas as pl
from jax.experimental.pallas import tpu as pltpu
from jax.sharding import PartitionSpec as P

LANES = 128
POWER = 64
FLOOR = 2.0 ** (-120.0 / POWER)
SCALE = 2.0 ** (120.0 / POWER) - FLOOR
LEAST = 2.0**-100


def encode(y, bound):
    code = jnp.abs(y) * (SCALE / bound) + FLOOR
    for _ in range(POWER.bit_length() - 1):
        code = code * code
    return jnp.where(y < 0, -code, code).astype(jnp.bfloat16)


def decode(code, bound):
    code = code.astype(jnp.float32)
    y = (jnp.exp(jnp.log(jnp.abs(code)) * (1.0 / POWER)) - FLOOR) * (bound * (1.0 / SCALE))
    return jnp.where(code < 0, -y, y)


def rounded_up(bound):
    return lax.reduce_precision(jnp.maximum(bound * (1.0 + 2.0**-6), LEAST), 8, 7)


def flips():
    return 0, 3, 2, 1


def column_block(width):
    units = width // LANES
    return LANES * max(d for d in range(1, min(units, 4) + 1) if units % d == 0)


def weight_copies(weights, target, sems, column, block):
    columns = pl.ds(pl.multiple_of(column * block, LANES), block)
    return [pltpu.make_async_copy(w.at[:, columns], target.at[i], sems.at[i]) for i, w in enumerate(weights)]


def fetch_kernel(all_blocks, block, gate_hbm, up_hbm, ahead_ref, sems):
    base = lax.axis_index("groups") * all_blocks
    copies = []
    for n in range(ahead_ref.shape[0]):
        copies += weight_copies((gate_hbm, up_hbm), ahead_ref.at[n], sems.at[n], base + n, block)
    for copy in copies:
        copy.start()
    for copy in copies:
        copy.wait()


def fetch(all_blocks, block, ahead, gate_weight, up_weight):
    depth = gate_weight.shape[0]
    return pl.pallas_call(
        functools.partial(fetch_kernel, all_blocks, block),
        in_specs=[pl.BlockSpec(memory_space=pl.ANY)] * 2,
        out_specs=pl.BlockSpec(memory_space=pltpu.VMEM),
        out_shape=jax.ShapeDtypeStruct((ahead, 2, depth, block), jnp.bfloat16),
        scratch_shapes=[pltpu.SemaphoreType.DMA((ahead, 2))],
        cost_estimate=pl.CostEstimate(flops=0, bytes_accessed=4 * depth * ahead * block, transcendentals=0),
        compiler_params=pltpu.CompilerParams(vmem_limit_bytes=16 << 20),
    )(gate_weight, up_weight)


def pick_rows(sizes, tokens, w):
    groups, gx, gy = sizes
    group, x, core = lax.axis_index("groups"), lax.axis_index("gx"), lax.axis_index("gy")
    rows = tokens.shape[0]
    each = rows // (groups * gx)
    held = rows // (groups * gy)
    quarter = rows // 4
    place = lax.broadcasted_iota(jnp.int32, (rows, rows), 0)
    source = lax.broadcasted_iota(jnp.int32, (rows, rows), 1)
    m = (place // quarter ^ w) * quarter + place % quarter
    j, q, i = m // (groups * each), (m // each) % groups, m % each
    steps = gx // 4
    part, flip = j // steps, jnp.zeros_like(j)
    for n in range(1, 4):
        flip = flip + jnp.where(part == n, flips()[n], 0)
    for n in range(2, gx.bit_length() - 1):
        steps //= 2
        flip = flip + j // steps % 2 * (1 << n)
    row = (x ^ flip) * each + i
    wanted = (q * gy + (row // held + gy - core) % gy) * held + row % held
    pick = (source == wanted).astype(jnp.bfloat16)
    return jnp.dot(pick, tokens, preferred_element_type=jnp.float32).astype(jnp.bfloat16)


def project_kernel(
    sizes, all_blocks, block, tokens_ref, ahead_ref, gate_hbm, up_hbm, keep_ref, *refs
):
    *send_refs, rows_ref, total_ref, buffer, sems = refs
    base = lax.axis_index("groups") * all_blocks
    slots = buffer.shape[0]
    ahead = ahead_ref.shape[0]
    later = all_blocks - ahead

    def copies(i, slot):
        return weight_copies((gate_hbm, up_hbm), buffer.at[slot], sems.at[slot], base + ahead + i, block)

    for i in range(min(slots - 1, later)):
        for copy in copies(i, i):
            copy.start()

    for w in range(2):
        rows_ref[w] = pick_rows(sizes, tokens_ref[...], w)
    high = total_ref.shape[3]
    tiles = block // LANES

    def multiply(n, w, weights):
        product = jnp.dot(rows_ref[w], weights, preferred_element_type=jnp.float32)
        for h in range(2):
            for t in range(tiles):
                total_ref[w, h, n * tiles + t] = product[h * high : (h + 1) * high, t * LANES : (t + 1) * LANES]

    for n in range(ahead):
        for w in range(2):
            multiply(n, w, ahead_ref[n, w])

    def step(n, carry):
        slot = lax.rem(n, slots)

        @pl.when(n + slots - 1 < later)
        def _():
            for copy in copies(n + slots - 1, lax.rem(n + slots - 1, slots)):
                copy.start()

        for w, copy in enumerate(copies(n, slot)):
            copy.wait()
            multiply(ahead + n, w, buffer[slot, w])
        return carry

    lax.fori_loop(0, later, step, 0)

    every = all_blocks * tiles
    spans = [slice(n * tiles, (n + 1) * tiles) for n in range(all_blocks)]
    first = lax.broadcasted_iota(jnp.int32, (tiles, high, LANES), 1) < high // 2
    for h in range(2):
        peaks = [jnp.zeros((high, LANES), jnp.float32)] * 2
        for span in spans:
            gate, up = total_ref[0, h, span], total_ref[1, h, span]
            parts = jnp.where(first, gate, up), pltpu.roll(jnp.where(first, up, gate), high // 2, 1)
            for i, part in enumerate(parts):
                total_ref[i, h, span] = part
                peaks[i] = jnp.maximum(peaks[i], jnp.max(jnp.abs(part), axis=0))
        for i in range(2):
            peak = jnp.broadcast_to(jnp.max(peaks[i], axis=1, keepdims=True), (high, LANES))
            bound = jnp.maximum(peak * (1.0 + 2.0**-6), LEAST).astype(jnp.bfloat16)
            exact = bound.astype(jnp.float32)
            if h == i == 0:
                keep_ref[every] = exact
                for span in spans:
                    keep_ref[span] = total_ref[i, h, span]
                continue
            send_ref = send_refs[2 * h + i - 1]
            send_ref[every] = bound
            for span in spans:
                send_ref[span] = encode(total_ref[i, h, span], exact[None])


def project(sizes, all_blocks, block, tokens, ahead, gate_weight, up_weight):
    rows, depth = tokens.shape
    width = all_blocks * block
    slots = 4
    shape = (width // LANES + 1, rows // 2, LANES)
    return pl.pallas_call(
        functools.partial(project_kernel, sizes, all_blocks, block),
        in_specs=[pl.BlockSpec(memory_space=pltpu.VMEM)] * 2 + [pl.BlockSpec(memory_space=pl.ANY)] * 2,
        out_specs=[pl.BlockSpec(memory_space=pltpu.VMEM)] * 4,
        out_shape=[jax.ShapeDtypeStruct(shape, jnp.float32)] + [jax.ShapeDtypeStruct(shape, jnp.bfloat16)] * 3,
        scratch_shapes=[
            pltpu.VMEM((2, rows, depth), jnp.bfloat16),
            pltpu.VMEM((2, 2, width // LANES, rows // 2, LANES), jnp.float32),
            pltpu.VMEM((slots, 2, depth, block), jnp.bfloat16),
            pltpu.SemaphoreType.DMA((slots, 2)),
        ],
        cost_estimate=pl.CostEstimate(
            flops=4 * rows * depth * width, bytes_accessed=4 * depth * width, transcendentals=0
        ),
        compiler_params=pltpu.CompilerParams(vmem_limit_bytes=32 << 20),
    )(tokens, ahead, gate_weight, up_weight)


def exchange(sizes, send, flip):
    groups, gx, gy = sizes
    pairs = [(x * gy + core, (x ^ flip(core)) * gy + core) for x in range(gx) for core in range(gy)]
    return lax.ppermute(send, ("gx", "gy"), pairs)


def opened(came):
    bound = came[-1:].astype(jnp.float32)
    return decode(came[:-1], bound), bound


def gather_rows(sizes, tokens):
    groups, gx, gy = sizes
    both = [
        (g * gy + core, (g + 1) % groups * gy + (core + 1) % gy) for g in range(groups) for core in range(gy)
    ]
    across = lax.ppermute(tokens, "groups", [(g, (g + 1) % groups) for g in range(groups)])
    diagonal = lax.ppermute(tokens, ("groups", "gy"), both)
    beside = lax.ppermute(tokens, "gy", [(core, (core + 1) % gy) for core in range(gy)])
    return jnp.concatenate([tokens, beside, across, diagonal], axis=0)


def per_device(sizes, tokens, gate_weight, up_weight):
    groups, gx, gy = sizes
    width = gate_weight.shape[1] // groups
    block = column_block(width)
    all_blocks = width // block
    ahead = fetch(all_blocks, block, min(3, all_blocks), gate_weight, up_weight)
    rows = gather_rows(sizes, tokens)
    keep, *sends = project(sizes, all_blocks, block, rows, ahead, gate_weight, up_weight)
    came = [exchange(sizes, send, lambda core: flips()[n + 1]) for n, send in enumerate(sends)]
    came = lax.optimization_barrier(came)
    total, bound = keep[:-1], keep[-1:]
    for part in came:
        value, part_bound = opened(part)
        total, bound = total + value, bound + part_bound
    shape = (2, total.shape[1] // 2, LANES)
    total, bound = total.reshape(-1, *shape), bound.reshape(-1, *shape)
    for n in range(2, gx.bit_length() - 1):
        half = total.shape[2] // 2
        bound = rounded_up(bound)
        send = encode(total[:, :, half:], bound[:, :, half:])
        send = jnp.concatenate([send, bound[:, :, half:].astype(jnp.bfloat16)], axis=0)
        value, part_bound = opened(exchange(sizes, send, lambda core: 1 << n))
        total, bound = total[:, :, :half] + value, bound[:, :, :half] + part_bound
    hidden = (jax.nn.silu(total[:, 0]) * total[:, 1]).astype(jnp.bfloat16)
    hidden = jnp.swapaxes(hidden, 0, 1).reshape(hidden.shape[1], width)
    each = hidden.shape[0] // groups
    own, theirs = hidden[:each], hidden[each:]
    theirs = lax.ppermute(theirs, "groups", [(g, (g + 1) % groups) for g in range(groups)])
    first = lax.axis_index("groups") == 0
    return jnp.concatenate([jnp.where(first, own, theirs), jnp.where(first, theirs, own)], axis=1)


def solution(mesh):
    sizes = tuple(mesh.shape[name] for name in ("groups", "gx", "gy"))
    in_specs = (P(("groups", "gy"), "gx"), P("gx", "gy"), P("gx", "gy"))
    out_specs = P(("groups", "gx"), "gy")
    return jax.shard_map(
        functools.partial(per_device, sizes), mesh=mesh, in_specs=in_specs, out_specs=out_specs, check_vma=False
    )
```

```python
import functools

import jax
import jax.numpy as jnp
from jax import lax
from jax.experimental import pallas as pl
from jax.experimental.pallas import tpu as pltpu
from jax.sharding import PartitionSpec as P

LANES = 128
POWER = 64
FLOOR = 2.0 ** (-120.0 / POWER)
SCALE = 2.0 ** (120.0 / POWER) - FLOOR
LEAST = 2.0**-100


def encode(y, bound):
    code = jnp.abs(y) * (SCALE / bound) + FLOOR
    for _ in range(POWER.bit_length() - 1):
        code = code * code
    return jnp.where(y < 0, -code, code).astype(jnp.bfloat16)


def decode(code, bound):
    code = code.astype(jnp.float32)
    y = (jnp.exp(jnp.log(jnp.abs(code)) * (1.0 / POWER)) - FLOOR) * (bound * (1.0 / SCALE))
    return jnp.where(code < 0, -y, y)


def rounded_up(bound):
    return lax.reduce_precision(jnp.maximum(bound * (1.0 + 2.0**-6), LEAST), 8, 7)


def flips():
    return 0, 3, 2, 1


def column_block(width):
    units = width // LANES
    return LANES * max(d for d in range(1, min(units, 4) + 1) if units % d == 0)


def weight_copies(weights, target, sems, column, block):
    columns = pl.ds(pl.multiple_of(column * block, LANES), block)
    return [pltpu.make_async_copy(w.at[:, columns], target.at[i], sems.at[i]) for i, w in enumerate(weights)]


def fetch_kernel(all_blocks, block, gate_hbm, up_hbm, ahead_ref, sems):
    base = lax.axis_index("groups") * all_blocks
    copies = []
    for n in range(ahead_ref.shape[0]):
        copies += weight_copies((gate_hbm, up_hbm), ahead_ref.at[n], sems.at[n], base + n, block)
    for copy in copies:
        copy.start()
    for copy in copies:
        copy.wait()


def fetch(all_blocks, block, ahead, gate_weight, up_weight):
    depth = gate_weight.shape[0]
    return pl.pallas_call(
        functools.partial(fetch_kernel, all_blocks, block),
        in_specs=[pl.BlockSpec(memory_space=pl.ANY)] * 2,
        out_specs=pl.BlockSpec(memory_space=pltpu.VMEM),
        out_shape=jax.ShapeDtypeStruct((ahead, 2, depth, block), jnp.bfloat16),
        scratch_shapes=[pltpu.SemaphoreType.DMA((ahead, 2))],
        cost_estimate=pl.CostEstimate(flops=0, bytes_accessed=4 * depth * ahead * block, transcendentals=0),
        compiler_params=pltpu.CompilerParams(vmem_limit_bytes=16 << 20),
    )(gate_weight, up_weight)


def pick_rows(sizes, tokens, w):
    groups, gx, gy = sizes
    group, x, core = lax.axis_index("groups"), lax.axis_index("gx"), lax.axis_index("gy")
    rows = tokens.shape[0]
    each = rows // (groups * gx)
    held = rows // (groups * gy)
    quarter, unit = rows // 4, groups * each
    place = lax.broadcasted_iota(jnp.int32, (rows, rows), 0)
    source = lax.broadcasted_iota(jnp.int32, (rows, rows), 1)
    odd = (place // unit) % 2 ^ w
    count = quarter // unit
    step = (place % (2 * quarter) // (2 * unit) + count - odd * w) % count
    m = (place // (2 * quarter) * 2 + odd) * quarter + step * unit + place % unit
    j, q, i = m // (groups * each), (m // each) % groups, m % each
    steps = gx // 4
    part, flip = j // steps, jnp.zeros_like(j)
    for n in range(1, 4):
        flip = flip + jnp.where(part == n, flips()[n], 0)
    for n in range(2, gx.bit_length() - 1):
        steps //= 2
        flip = flip + j // steps % 2 * (1 << n)
    row = (x ^ flip) * each + i
    wanted = (q * gy + (row // held + gy - core) % gy) * held + row % held
    pick = (source == wanted).astype(jnp.bfloat16)
    return jnp.dot(pick, tokens, preferred_element_type=jnp.float32).astype(jnp.bfloat16)


def project_kernel(
    sizes, all_blocks, block, tokens_ref, ahead_ref, gate_hbm, up_hbm, keep_ref, *refs
):
    *send_refs, rows_ref, total_ref, buffer, sems = refs
    base = lax.axis_index("groups") * all_blocks
    slots = buffer.shape[0]
    ahead = ahead_ref.shape[0]
    later = all_blocks - ahead

    def copies(i, slot):
        return weight_copies((gate_hbm, up_hbm), buffer.at[slot], sems.at[slot], base + ahead + i, block)

    for i in range(min(slots - 1, later)):
        for copy in copies(i, i):
            copy.start()

    for w in range(2):
        rows_ref[w] = pick_rows(sizes, tokens_ref[...], w)
    high = total_ref.shape[3]
    tiles = block // LANES

    def multiply(n, w, weights):
        product = jnp.dot(rows_ref[w], weights, preferred_element_type=jnp.float32)
        for h in range(2):
            for t in range(tiles):
                total_ref[w, h, n * tiles + t] = product[h * high : (h + 1) * high, t * LANES : (t + 1) * LANES]

    unit = sizes[0] * (2 * high // (sizes[0] * sizes[1]))
    first = lax.broadcasted_iota(jnp.int32, (tiles, high, LANES), 1) // unit % 2 == 0

    def arrange(n, peaks):
        span = pl.ds(n * tiles, tiles)
        peaks = list(peaks)
        for h in range(2):
            gate, up = total_ref[0, h, span], total_ref[1, h, span]
            parts = jnp.where(first, gate, up), pltpu.roll(jnp.where(first, up, gate), high - unit, 1)
            for i, part in enumerate(parts):
                total_ref[i, h, span] = part
                peaks[2 * h + i] = jnp.maximum(peaks[2 * h + i], jnp.max(jnp.abs(part), axis=0))
        return tuple(peaks)

    for n in range(ahead):
        for w in range(2):
            multiply(n, w, ahead_ref[n, w])

    def step(n, peaks):
        slot = lax.rem(n, slots)

        @pl.when(n + slots - 1 < later)
        def _():
            for copy in copies(n + slots - 1, lax.rem(n + slots - 1, slots)):
                copy.start()

        peaks = arrange(ahead + n - 1, peaks)
        for w, copy in enumerate(copies(n, slot)):
            copy.wait()
            multiply(ahead + n, w, buffer[slot, w])
        return peaks

    peaks = (jnp.zeros((high, LANES), jnp.float32),) * 4
    for n in range(ahead - 1):
        peaks = arrange(n, peaks)
    peaks = lax.fori_loop(0, later, step, peaks)
    peaks = arrange(all_blocks - 1, peaks)

    every = all_blocks * tiles
    for i in range(4):
        done_ref = total_ref.at[i % 2, i // 2]
        peak = jnp.broadcast_to(jnp.max(peaks[i], axis=1, keepdims=True), (high, LANES))
        bound = jnp.maximum(peak * (1.0 + 2.0**-6), LEAST).astype(jnp.bfloat16)
        exact = bound.astype(jnp.float32)
        if i == 0:
            keep_ref[every] = exact
        else:
            send_refs[i - 1][every] = bound
        for n in range(all_blocks):
            span = slice(n * tiles, (n + 1) * tiles)
            if i == 0:
                keep_ref[span] = done_ref[span]
            else:
                send_refs[i - 1][span] = encode(done_ref[span], exact[None])


def project(sizes, all_blocks, block, tokens, ahead, gate_weight, up_weight):
    rows, depth = tokens.shape
    width = all_blocks * block
    slots = 4
    shape = (width // LANES + 1, rows // 2, LANES)
    return pl.pallas_call(
        functools.partial(project_kernel, sizes, all_blocks, block),
        in_specs=[pl.BlockSpec(memory_space=pltpu.VMEM)] * 2 + [pl.BlockSpec(memory_space=pl.ANY)] * 2,
        out_specs=[pl.BlockSpec(memory_space=pltpu.VMEM)] * 4,
        out_shape=[jax.ShapeDtypeStruct(shape, jnp.float32)] + [jax.ShapeDtypeStruct(shape, jnp.bfloat16)] * 3,
        scratch_shapes=[
            pltpu.VMEM((2, rows, depth), jnp.bfloat16),
            pltpu.VMEM((2, 2, width // LANES, rows // 2, LANES), jnp.float32),
            pltpu.VMEM((slots, 2, depth, block), jnp.bfloat16),
            pltpu.SemaphoreType.DMA((slots, 2)),
        ],
        cost_estimate=pl.CostEstimate(
            flops=4 * rows * depth * width, bytes_accessed=4 * depth * width, transcendentals=0
        ),
        compiler_params=pltpu.CompilerParams(vmem_limit_bytes=32 << 20),
    )(tokens, ahead, gate_weight, up_weight)


def exchange(sizes, send, flip):
    groups, gx, gy = sizes
    pairs = [(x * gy + core, (x ^ flip(core)) * gy + core) for x in range(gx) for core in range(gy)]
    return lax.ppermute(send, ("gx", "gy"), pairs)


def opened(came):
    plain = came.astype(jnp.float32)
    last = lax.broadcasted_iota(jnp.int32, came.shape, 0) == came.shape[0] - 1
    return jnp.where(last, plain, decode(came, plain[-1:]))


def coded(sums, bound):
    bound = rounded_up(bound)
    last = lax.broadcasted_iota(jnp.int32, sums.shape, 0) == sums.shape[0] - 1
    return jnp.where(last, jnp.broadcast_to(bound, sums.shape).astype(jnp.bfloat16), encode(sums, bound))


def gather_rows(sizes, tokens):
    groups, gx, gy = sizes
    both = [
        (g * gy + core, (g + 1) % groups * gy + (core + 1) % gy) for g in range(groups) for core in range(gy)
    ]
    across = lax.ppermute(tokens, "groups", [(g, (g + 1) % groups) for g in range(groups)])
    diagonal = lax.ppermute(tokens, ("groups", "gy"), both)
    beside = lax.ppermute(tokens, "gy", [(core, (core + 1) % gy) for core in range(gy)])
    return jnp.concatenate([tokens, beside, across, diagonal], axis=0)


def per_device(sizes, tokens, gate_weight, up_weight):
    groups, gx, gy = sizes
    width = gate_weight.shape[1] // groups
    block = column_block(width)
    all_blocks = width // block
    ahead = fetch(all_blocks, block, min(3, all_blocks), gate_weight, up_weight)
    rows = gather_rows(sizes, tokens)
    keep, *sends = project(sizes, all_blocks, block, rows, ahead, gate_weight, up_weight)
    came = [exchange(sizes, send, lambda core: flips()[n + 1]) for n, send in enumerate(sends)]
    keep, *came = lax.optimization_barrier((keep, *came))
    parts = [keep, *came]
    for n in range(2, gx.bit_length() - 1):
        half = parts[0].shape[1] // 2
        send = [part[:, half:] for part in parts]
        bound = sum(part[-1:].astype(jnp.float32) for part in send)
        send = coded(sum((opened(part) for part in send[1:]), send[0]), bound)
        send, *parts = lax.optimization_barrier((send, *parts))
        came = exchange(sizes, send, lambda core: 1 << n)
        keep = [part[:, :half] for part in parts]
        keep = sum((opened(part) for part in keep[1:]), keep[0])
        parts = lax.optimization_barrier((keep, came))
    total = sum((opened(part) for part in parts[1:]), parts[0])[:-1]
    half = total.shape[1] // 2
    hidden = (jax.nn.silu(total[:, :half]) * total[:, half:]).astype(jnp.bfloat16)
    hidden = jnp.swapaxes(hidden, 0, 1).reshape(hidden.shape[1], width)
    each = hidden.shape[0] // groups
    own, theirs = hidden[:each], hidden[each:]
    theirs = lax.ppermute(theirs, "groups", [(g, (g + 1) % groups) for g in range(groups)])
    first = lax.axis_index("groups") == 0
    return jnp.concatenate([jnp.where(first, own, theirs), jnp.where(first, theirs, own)], axis=1)


def solution(mesh):
    sizes = tuple(mesh.shape[name] for name in ("groups", "gx", "gy"))
    in_specs = (P(("groups", "gy"), "gx"), P("gx", "gy"), P("gx", "gy"))
    out_specs = P(("groups", "gx"), "gy")
    return jax.shard_map(
        functools.partial(per_device, sizes), mesh=mesh, in_specs=in_specs, out_specs=out_specs, check_vma=False
    )
```
